32 devices in a mesh: grid: 16 (over z, y, x), col: 2 (over core).
Axes of the slice: x: 2, y: 2, z: 4, core: 2. Of those that a mesh axis runs over, the one named last changes fastest.
Arguments:
- density: bfloat16 [49152, 256], P('grid', 'col'), may hold values from -0.029907227 to 0.029907227
- row_centers: float32 [3, 49152], P(None, 'grid'), may hold values from -2 to 2
- row_exps: float32 [49152], P('grid'), may hold values from 0.2 to 1
- win_centers: float32 [3, 256], P(None, 'col'), may hold values from -2 to 2
- win_exps: float32 [256], P('col'), may hold values from 0.2 to 1
- points: float32 [64, 3, 128], P('grid'), may hold values from -2 to 2
- weights: float32 [64, 128], P('grid'), may hold values from 0.05 to 0.5
- sig_blocks: int32 [64, 32], replicated, may hold values from 0 to 383, as said below
- pair_target: int32 [64, 4096], P('grid', 'col'), may hold values from 0 to 255
- pair_source: int32 [64, 4096], P('grid', 'col'), may hold values from 0 to 127
Outputs:
- fock: float32 [49152, 256], P('grid', 'col')
The draws below stay inside these ranges and needn't reach their ends.
Inputs may be any that keep to these rules, and one draw needn't show every extreme that they name: `sig_blocks`: each row lists 32 different blocks; block i is owned by grid index i // 24. Over the 4 rows of one grid index d (rows d * 4 to (d + 1) * 4 - 1, the batches that index holds), at most 2 different blocks of any one owner appear, and exactly 2 for some owner.
All inputs are finite; a program needn't handle non-finite values.
Results may differ from the reference program's by a relative error of at most 0.0011.
Values may be sent and summed in bfloat16 or wider, within the bound.
A program may use at most 64 MiB of HBM per device.

```python
import math
import jax
import jax.numpy as jnp
from jax import lax

BLK = 128
PTS = 128
CAPB = 2
BLK_DEV = 24
S = 32
BPD = 4
COLW_DEV = 128
NBF = 49152
NCOLW = 256
BATCHES = 64
NPAIR_ALL = 4096
N_GRID = 16
N_COL = 2


def draw_sig_blocks(key, part):
    owner_key, batch_key = jax.random.split(jax.random.fold_in(key, 11))
    owner_scores = jax.random.randint(owner_key, (N_GRID, N_GRID, BLK_DEV), 0, 2 ** 20) * BLK_DEV + jnp.arange(BLK_DEV, dtype=jnp.int32)
    chosen_local = jnp.argsort(owner_scores, axis=2)[:, :, :CAPB]
    pool = chosen_local + (jnp.arange(N_GRID, dtype=jnp.int32) * BLK_DEV)[None, :, None]
    pool_size = CAPB * N_GRID
    pool = pool.reshape(N_GRID, pool_size)
    positions = jnp.arange(pool_size, dtype=jnp.int32)
    pick_scores = jax.random.randint(batch_key, (N_GRID, BPD, pool_size), 0, 2 ** 20) * pool_size + positions[None, None, :]
    next_owner = (jnp.arange(N_GRID, dtype=jnp.int32) + 1) % N_GRID
    forced = positions[None, :] // CAPB == next_owner[:, None]
    first_batch = jnp.arange(BPD, dtype=jnp.int32) == 0
    forced_all = forced[:, None, :] & first_batch[None, :, None]
    pick_scores = jnp.where(forced_all, -1 - positions[None, None, :] % CAPB, pick_scores)
    order = jnp.argsort(pick_scores, axis=2)[:, :, :S]
    pool_wide = jnp.broadcast_to(pool[:, None, :], (N_GRID, BPD, pool_size))
    chosen = jnp.take_along_axis(pool_wide, order, axis=2)
    return chosen.reshape(N_GRID * BPD, S).astype(jnp.int32)


def plant(values, stream_key, least, high):
    longest = values.shape.index(max(values.shape))
    spots = []
    for shift in (0, 1):
        where = [jax.random.randint(jax.random.fold_in(stream_key, axis), (), 0, length) for axis, length in enumerate(values.shape)]
        where[longest] = (where[longest] + shift) % values.shape[longest]
        spots.append(tuple(where))
    return values.at[spots[0]].set(least).at[spots[1]].set(high)


def block_scale(key, dims, cuts, least, largest):
    factor_of, own = 1.0, jax.random.fold_in(key, 6)
    for axis_at, parts in cuts:
        draws = jnp.exp(jax.random.uniform(jax.random.fold_in(own, axis_at), (parts,), jnp.float32, least / len(cuts), largest / len(cuts)))
        factor_of = factor_of * jnp.repeat(draws, dims[axis_at] // parts).reshape([-1 if axis == axis_at else 1 for axis in range(len(dims))])
    return factor_of


def noise(key, dims, width, bound, shards=(), held_as=jnp.bfloat16):
    values = width * jax.random.normal(key, dims, jnp.float32)
    if shards:
        values = values * block_scale(key, dims, shards, -0.22, 0.18)
    return jnp.clip(values, -bound, bound).astype(held_as)


def setup_inputs(seed: int = 0) -> dict:
    splits = jax.random.split(jax.random.key(seed), 11)
    return {
        "density": noise(splits[0], (NBF, NCOLW), 0.005, 0.029907227, ((0, 16), (1, 2))),
        "row_centers": jnp.clip(jax.random.uniform(splits[1], (3, NBF), jnp.float32, -2.0, 2.0) * block_scale(splits[1], (3, NBF), ((1, 16),), -0.4, 0.0), -2.0, 2.0),
        "row_exps": jnp.clip(jnp.exp(math.log(1.0) - 1.609438 * jax.random.uniform(splits[2], (NBF,), jnp.float32) ** block_scale(splits[2], (NBF,), ((0, 16),), -0.2, 0.2)), 0.2, 1.0),
        "win_centers": jnp.clip(jax.random.uniform(splits[3], (3, NCOLW), jnp.float32, -2.0, 2.0) * block_scale(splits[3], (3, NCOLW), ((1, 2),), -0.4, 0.0), -2.0, 2.0),
        "win_exps": jnp.clip(jnp.exp(math.log(1.0) - 1.609438 * jax.random.uniform(splits[4], (NCOLW,), jnp.float32) ** block_scale(splits[4], (NCOLW,), ((0, 2),), -0.2, 0.2)), 0.2, 1.0),
        "points": jnp.clip(jax.random.uniform(splits[5], (BATCHES, 3, PTS), jnp.float32, -2.0, 2.0) * block_scale(splits[5], (BATCHES, 3, PTS), ((0, 16),), -0.4, 0.0), -2.0, 2.0),
        "weights": jnp.clip(jnp.exp(math.log(0.5) - 2.3025851 * jax.random.uniform(splits[6], (BATCHES, PTS), jnp.float32) ** block_scale(splits[6], (BATCHES, PTS), ((0, 16),), -0.2, 0.2)), 0.05, 0.5),
        "sig_blocks": draw_sig_blocks(jax.random.fold_in(splits[10], 71), 0),
        "pair_target": plant(jax.random.randint(splits[8], (BATCHES, NPAIR_ALL), 0, NCOLW), jax.random.fold_in(splits[8], 1), 0, NCOLW - 1).astype(jnp.int32),
        "pair_source": plant(jax.random.randint(splits[9], (BATCHES, NPAIR_ALL), 0, COLW_DEV), jax.random.fold_in(splits[9], 1), 0, COLW_DEV - 1).astype(jnp.int32),
    }


quad_nodes = 8


def boys_zero(argument):
    summed = jnp.zeros_like(argument)
    for quad_node in range(quad_nodes):
        node_spot = (quad_node + 0.5) / quad_nodes
        summed = summed + jnp.exp(-argument * (node_spot * node_spot))
    return summed / quad_nodes


def basis_values(centers, exponents, coordinates):
    squared = None
    for axis_id in range(3):
        deltas = coordinates[..., axis_id, :, None] - centers[..., axis_id, None, :]
        squared = deltas * deltas if squared is None else squared + deltas * deltas
    return jnp.exp(-exponents[..., None, :] * squared)


def pair_values(target_par, source_par, coordinates):
    target_exp = target_par[..., 3, :]
    source_exp = source_par[..., 3, :]
    joined = target_exp + source_exp
    separation = jnp.zeros_like(joined)
    spread = None
    for axis_id in range(3):
        offset = target_par[..., axis_id, :] - source_par[..., axis_id, :]
        separation = separation + offset * offset
        centre = (target_exp * target_par[..., axis_id, :] + source_exp * source_par[..., axis_id, :]) / joined
        deltas = coordinates[..., axis_id, :, None] - centre[..., None, :]
        spread = deltas * deltas if spread is None else spread + deltas * deltas
    prefactor = (2.0 * math.pi / joined) * jnp.exp(-target_exp * source_exp / joined * separation)
    return prefactor[..., None, :] * boys_zero(joined[..., None, :] * spread)


def reference(density, row_centers, row_exps, win_centers, win_exps, points, weights, sig_blocks, pair_target, pair_source):
    window = jnp.concatenate([win_centers, win_exps[None, :]], axis=0)
    row_params = jnp.concatenate([row_centers, row_exps[None, :]], axis=0)
    column_count = density.shape[1]
    local_width = column_count // N_COL
    per_column = pair_target.shape[1] // N_COL
    source_global = pair_source + (jnp.arange(pair_target.shape[1], dtype=jnp.int32) // per_column * local_width)[None, :]

    def one_batch(fock_sum, inputs):
        listing, coordinates, point_weights, target, source = inputs
        row_ids = (listing[:, None] * BLK + jnp.arange(BLK, dtype=jnp.int32)[None, :]).reshape(-1).astype(jnp.int32)
        row_tiles = jnp.take(density, row_ids, axis=0).astype(jnp.float32)
        params = jnp.take(row_params, row_ids, axis=1)
        basis_rows = basis_values(params[0:3], params[3], coordinates).astype(jnp.bfloat16)
        field_values = jnp.dot(basis_rows.astype(jnp.float32), row_tiles, preferred_element_type=jnp.float32, precision=lax.Precision.HIGHEST).astype(jnp.bfloat16)
        target_par = jnp.take(window, target, axis=1)
        source_par = jnp.take(window, source, axis=1)
        field_source = jnp.take(field_values, source, axis=1).astype(jnp.float32)
        product = (pair_values(target_par, source_par, coordinates) * field_source).astype(jnp.bfloat16)
        potential = jnp.zeros((coordinates.shape[1], column_count), jnp.float32).at[:, target].add(product.astype(jnp.float32))
        weighted = (point_weights[:, None] * potential).astype(jnp.bfloat16)
        contribution = jnp.dot(basis_rows.astype(jnp.float32).T, weighted.astype(jnp.float32), preferred_element_type=jnp.float32, precision=lax.Precision.HIGHEST)
        return fock_sum.at[row_ids].add(contribution), None

    zero_fock = jnp.zeros(density.shape, jnp.float32)
    fock_sum, unused = lax.scan(one_batch, zero_fock, (sig_blocks, points, weights, pair_target, source_global))
    return fock_sum
```

```python
import functools
import math

import jax
import jax.numpy as jnp
from jax import lax
from jax.experimental import pallas as pl
from jax.experimental.pallas import tpu as pltpu
from jax.sharding import PartitionSpec as P

BLK = 128
CAPB = 2
MESH = pl.DeviceIdType.MESH
VMEM_LIMIT = 52 * 1024 * 1024

quad_nodes = 8


def boys_sum(argument):
    first = jnp.exp(argument * (-0.25 / (quad_nodes * quad_nodes)))
    ratio = jnp.exp(argument * (-2.0 / (quad_nodes * quad_nodes)))
    powers = [ratio]
    for _ in range(quad_nodes - 2):
        powers.append(powers[-1] * ratio)
    summed = 1.0 + powers[-1]
    for power in powers[-2::-1]:
        summed = 1.0 + power * summed
    return first * summed


def three_pieces(values):
    high = values.astype(jnp.bfloat16).astype(jnp.float32)
    rest = values - high
    middle = rest.astype(jnp.bfloat16).astype(jnp.float32)
    return jnp.concatenate([high, middle, rest - middle], axis=0).astype(jnp.bfloat16)


def picked(pieces, pick):
    out = jnp.dot(pieces, pick, preferred_element_type=jnp.float32)
    return out[0:8] + out[8:16] + out[16:24]


def one_hot(ids, count):
    rows = lax.broadcasted_iota(jnp.int32, (count, ids.shape[1]), 0)
    return jnp.where(rows == ids, 1.0, 0.0).astype(jnp.bfloat16)


def exchange_kernel(
    owners, cols, full,
    slot_ref, mask_ref, density_ref, params_ref, win_c_ref, win_e_ref, points_ref, weights_ref,
    target_ref, source_ref,
    weighted_ref, all_points_ref,
    tile_send, tile_recv, msg_send, msg_recv, win_buf, spots, pair_scr, source_hot, target_hot, field, parts, parts_recv,
    tile_ss, tile_rs, msg_ss, msg_rs, win_ss, win_rs, part_ss, part_rs,
):
    me = lax.axis_index("grid")
    mc = lax.axis_index("col")
    batches, pairs = target_ref.shape
    pts = points_ref.shape[2]
    width = density_ref.shape[2]
    window = cols * width
    chunk = 256

    barrier = pltpu.get_barrier_semaphore()

    def greet_grid(j, carry):
        pl.semaphore_signal(
            barrier, inc=1, device_id={"grid": lax.rem(me + j, owners), "col": mc}, device_id_type=MESH
        )
        return carry

    def greet_col(j, carry):
        pl.semaphore_signal(
            barrier, inc=1, device_id={"grid": me, "col": lax.rem(mc + j, cols)}, device_id_type=MESH
        )
        return carry

    lax.fori_loop(1, owners, greet_grid, 0)
    lax.fori_loop(1, cols, greet_col, 0)

    def win_copy(j):
        return pltpu.make_async_remote_copy(
            src_ref=win_buf.at[mc], dst_ref=win_buf.at[mc], send_sem=win_ss.at[j], recv_sem=win_rs.at[j],
            device_id={"grid": me, "col": lax.rem(mc + j, cols)}, device_id_type=MESH,
        )

    def win_arrival(j):
        there = lax.rem(mc - j + cols, cols)
        return pltpu.make_async_remote_copy(
            src_ref=win_buf.at[there], dst_ref=win_buf.at[there], send_sem=win_ss.at[j], recv_sem=win_rs.at[j],
            device_id={"grid": me, "col": lax.rem(mc + j, cols)}, device_id_type=MESH,
        )

    def msg_copy(j):
        return pltpu.make_async_remote_copy(
            src_ref=msg_send.at[j], dst_ref=msg_recv.at[j], send_sem=msg_ss.at[j], recv_sem=msg_rs.at[j],
            device_id={"grid": lax.rem(me + j, owners), "col": mc}, device_id_type=MESH,
        )

    def tile_copy(j):
        return pltpu.make_async_remote_copy(
            src_ref=tile_send.at[j], dst_ref=tile_recv.at[j], send_sem=tile_ss.at[j], recv_sem=tile_rs.at[j],
            device_id={"grid": lax.rem(me + j, owners), "col": mc}, device_id_type=MESH,
        )

    def part_copy(j):
        there = lax.rem(mc + j, cols)
        return pltpu.make_async_remote_copy(
            src_ref=parts.at[there], dst_ref=parts_recv.at[j], send_sem=part_ss.at[j], recv_sem=part_rs.at[j],
            device_id={"grid": me, "col": there}, device_id_type=MESH,
        )

    own_win = jnp.concatenate([win_c_ref[...], win_e_ref[...], jnp.zeros((4, width), jnp.float32)], axis=0)
    win_buf[mc] = own_win
    own_points = jnp.concatenate([points_ref[b] for b in range(batches)] + [weights_ref[...]], axis=0)

    def stage(j, tile_to, msg_to, index):
        peer = lax.rem(me + j, owners)
        rows = []
        for c in range(CAPB):
            block = slot_ref[peer * CAPB + c]
            tile_to[index, c * BLK : (c + 1) * BLK] = density_ref[block]
            rows.append(params_ref[block])
        msg_to[index] = jnp.concatenate(rows + [own_points], axis=0)

    stage(0, tile_recv, msg_recv, 0)
    pl.semaphore_wait(barrier, owners - 1 + cols - 1)

    for j in range(1, cols):
        win_copy(j).start()

    def send(j, carry):
        stage(j, tile_send, msg_send, j)
        msg_copy(j).start()
        tile_copy(j).start()
        return carry

    lax.fori_loop(1, owners, send, 0)

    columns = own_points.T
    for b in range(batches):
        for a in range(3):
            spots[a, b * pts : (b + 1) * pts] = jnp.broadcast_to(columns[:, 3 * b + a : 3 * b + a + 1], (pts, BLK))
        at = 3 * batches + b
        spots[3, b * pts : (b + 1) * pts] = jnp.broadcast_to(columns[:, at : at + 1], (pts, BLK))

    for j in range(1, cols):
        win_arrival(j).wait_recv()
    source_pieces = three_pieces(own_win)
    target_pieces = three_pieces(jnp.concatenate([win_buf[k] for k in range(cols)], axis=1))
    per_batch = pairs // chunk

    def pair_step(i, carry):
        b = i // per_batch
        lanes = pl.ds(pl.multiple_of(lax.rem(i, per_batch) * chunk, chunk), chunk)
        rows = pl.ds(pl.multiple_of(b * pts, pts), pts)
        target_pick = one_hot(target_ref[pl.ds(b, 1), lanes], window)
        source_pick = one_hot(source_ref[pl.ds(b, 1), lanes], width)
        target_hot[b, :, lanes] = target_pick
        source_hot[b, :, lanes] = source_pick
        tp = picked(target_pieces, target_pick)
        sp = picked(source_pieces, source_pick)
        te, se = tp[3:4], sp[3:4]
        joined = te + se
        separation = jnp.zeros_like(joined)
        centre = []
        for a in range(3):
            offset = tp[a : a + 1] - sp[a : a + 1]
            separation = separation + offset * offset
            centre.append((te * tp[a : a + 1] + se * sp[a : a + 1]) / joined)
        prefactor = (2.0 * math.pi / quad_nodes) / joined * jnp.exp(-te * se / joined * separation)
        out = []
        for h in range(chunk // BLK):
            part = slice(h * BLK, (h + 1) * BLK)
            spread = None
            for a in range(3):
                deltas = spots[a, rows] - centre[a][:, part]
                spread = deltas * deltas if spread is None else spread + deltas * deltas
            out.append(prefactor[:, part] * boys_sum(joined[:, part] * spread))
        pair_scr[rows, lanes] = jnp.concatenate(out, axis=1)
        return carry

    lax.fori_loop(0, batches * per_batch, pair_step, 0)

    field[...] = jnp.zeros_like(field)

    def add_field(j):
        owner = lax.rem(me - j + owners, owners)
        params = msg_recv[j]
        all_points_ref[owner] = params[8:24]
        tile = tile_recv[j]
        for b in range(batches):
            rows = slice(b * pts, (b + 1) * pts)
            halves = []
            for c in range(CAPB):
                squared = None
                for a in range(3):
                    deltas = spots[a, rows] - params[4 * c + a : 4 * c + a + 1]
                    squared = deltas * deltas if squared is None else squared + deltas * deltas
                value = jnp.exp(-params[4 * c + 3 : 4 * c + 4] * squared)
                if not full:
                    value = value * mask_ref[(b * owners + owner) * CAPB + c]
                halves.append(value.astype(jnp.bfloat16))
            basis = jnp.concatenate(halves, axis=1)
            field[rows] += jnp.dot(basis, tile, preferred_element_type=jnp.float32)

    add_field(0)

    def take(j, carry):
        msg_copy(j).wait_recv()
        tile_copy(j).wait_recv()
        add_field(j)
        return carry

    lax.fori_loop(1, owners, take, 0)

    def batch_step(b, carry):
        rows = pl.ds(pl.multiple_of(b * pts, pts), pts)
        values = field[rows].astype(jnp.bfloat16)
        total = jnp.zeros((pts, window), jnp.float32)
        for i in range(per_batch // 2):
            lanes = slice(i * 2 * chunk, (i + 1) * 2 * chunk)
            from_field = jnp.dot(values, source_hot[b, :, lanes], preferred_element_type=jnp.float32)
            product = (pair_scr[rows, lanes] * from_field).astype(jnp.bfloat16)
            total = total + lax.dot_general(
                product, target_hot[b, :, lanes], (((1,), (1,)), ((), ())), preferred_element_type=jnp.float32
            )
        for k in range(cols):
            parts[k, rows] = total[:, k * width : (k + 1) * width]
        return carry

    lax.fori_loop(0, batches, batch_step, 0)

    for j in range(1, cols):
        part_copy(j).start()
    for j in range(1, cols):
        part_copy(j).wait_recv()
    potential = parts[mc]
    for j in range(1, cols):
        potential = potential + parts_recv[j]
    weighted_ref[...] = (spots[3] * potential).astype(jnp.bfloat16)

    for j in range(1, cols):
        win_copy(j).wait_send()
        part_copy(j).wait_send()

    def drain(j, carry):
        msg_copy(j).wait_send()
        tile_copy(j).wait_send()
        return carry

    lax.fori_loop(1, owners, drain, 0)


def fock_kernel(owners, batches, full, slot_ref, mask_ref, weighted_ref, points_ref, params_ref, fock_ref):
    fock_ref[...] = jnp.zeros_like(fock_ref)
    count = weighted_ref.shape[0] // owners
    blank = jnp.zeros((4, BLK), jnp.float32)

    def step(user, carry):
        weighted = weighted_ref[pl.ds(pl.multiple_of(user * count, count), count), :]
        spot = points_ref[user]
        for c in range(CAPB):
            block = slot_ref[user * CAPB + c]
            params = jnp.concatenate([params_ref[block], blank], axis=0).T
            held = [jnp.broadcast_to(params[:, a : a + 1], (BLK, BLK)) for a in range(4)]
            basis = []
            for b in range(batches):
                squared = None
                for a in range(3):
                    deltas = spot[3 * b + a : 3 * b + a + 1] - held[a]
                    squared = deltas * deltas if squared is None else squared + deltas * deltas
                value = jnp.exp(-held[3] * squared)
                if not full:
                    value = value * mask_ref[(user * CAPB + c) * batches + b]
                basis.append(value.astype(jnp.bfloat16))
            fock_ref[block] += jnp.dot(
                jnp.concatenate(basis, axis=1), weighted, preferred_element_type=jnp.float32
            )
        return carry

    lax.fori_loop(0, owners, step, 0)


def on_device(
    density, row_centers, row_exps, win_centers, win_exps, points, weights, sig_blocks, pair_target, pair_source
):
    owners = lax.axis_size("grid")
    cols = lax.axis_size("col")
    me = lax.axis_index("grid")
    rows_here = row_exps.shape[0]
    held = rows_here // BLK
    width = density.shape[1]
    batches, _, pts = points.shape
    pairs = pair_target.shape[1]
    listed = sig_blocks.shape[1]
    full = listed == owners * CAPB
    count = batches * pts

    lists = sig_blocks.reshape(owners, batches * listed)
    local = lists - me * held
    mine = (local >= 0) & (local < held)
    low = jnp.min(jnp.where(mine, local, held), axis=1)
    high = jnp.max(jnp.where(mine, local, -1), axis=1)
    slots = jnp.clip(jnp.stack([low, high], axis=1), 0, held - 1).reshape(-1)
    if full:
        user_mask = owner_mask = jnp.zeros((1,), jnp.float32)
    else:
        my_lists = lax.dynamic_slice_in_dim(sig_blocks, me * batches, batches, 0)
        flat = my_lists.reshape(1, -1)
        of_owner = flat // held == jnp.arange(owners, dtype=jnp.int32)[:, None]
        least = jnp.min(jnp.where(of_owner, flat, owners * held), axis=1)
        most = jnp.max(jnp.where(of_owner, flat, -1), axis=1)
        most = jnp.where(most == least, -1, most)
        wanted = jnp.stack([least, most], axis=1)
        user_mask = jnp.any(my_lists[:, :, None, None] == wanted, axis=1).astype(jnp.float32).reshape(-1)
        ids = jnp.stack([low, jnp.where(high == low, -1, high)], axis=1)
        ids = jnp.where((ids >= 0) & (ids < held), ids + me * held, -1)
        by_batch = sig_blocks.reshape(owners, 1, batches, listed)
        owner_mask = jnp.any(by_batch == ids[:, :, None, None], axis=3).astype(jnp.float32).reshape(-1)

    smem = pl.BlockSpec(memory_space=pltpu.SMEM)
    vmem = pl.BlockSpec(memory_space=pltpu.VMEM)
    own_tiles = density.reshape(held, BLK, width)
    params = jnp.concatenate([row_centers, row_exps[None, :]], axis=0).reshape(4, held, BLK).transpose(1, 0, 2)
    weighted, all_points = pl.pallas_call(
        functools.partial(exchange_kernel, owners, cols, full),
        out_shape=(
            jax.ShapeDtypeStruct((count, width), jnp.bfloat16),
            jax.ShapeDtypeStruct((owners, 16, pts), jnp.float32),
        ),
        in_specs=[smem, smem] + [vmem] * 8,
        out_specs=(vmem, vmem),
        scratch_shapes=[
            pltpu.VMEM((owners, CAPB * BLK, width), jnp.bfloat16),
            pltpu.VMEM((owners, CAPB * BLK, width), jnp.bfloat16),
            pltpu.VMEM((owners, 24, BLK), jnp.float32),
            pltpu.VMEM((owners, 24, BLK), jnp.float32),
            pltpu.VMEM((cols, 8, width), jnp.float32),
            pltpu.VMEM((4, count, BLK), jnp.float32),
            pltpu.VMEM((count, pairs), jnp.float32),
            pltpu.VMEM((batches, width, pairs), jnp.bfloat16),
            pltpu.VMEM((batches, cols * width, pairs), jnp.bfloat16),
            pltpu.VMEM((count, width), jnp.float32),
            pltpu.VMEM((cols, count, width), jnp.float32),
            pltpu.VMEM((cols, count, width), jnp.float32),
            pltpu.SemaphoreType.DMA((owners,)),
            pltpu.SemaphoreType.DMA((owners,)),
            pltpu.SemaphoreType.DMA((owners,)),
            pltpu.SemaphoreType.DMA((owners,)),
            pltpu.SemaphoreType.DMA((cols,)),
            pltpu.SemaphoreType.DMA((cols,)),
            pltpu.SemaphoreType.DMA((cols,)),
            pltpu.SemaphoreType.DMA((cols,)),
        ],
        compiler_params=pltpu.CompilerParams(
            collective_id=0, has_side_effects=True, vmem_limit_bytes=VMEM_LIMIT
        ),
        name="exchange",
    )(
        slots, user_mask, own_tiles, params, win_centers, win_exps[None, :], points, weights,
        pair_target, pair_source,
    )
    every = lax.all_gather(weighted, "grid", axis=0, tiled=True)
    return pl.pallas_call(
        functools.partial(fock_kernel, owners, batches, full),
        out_shape=jax.ShapeDtypeStruct((held, BLK, width), jnp.float32),
        in_specs=[smem, smem] + [vmem] * 3,
        out_specs=vmem,
        compiler_params=pltpu.CompilerParams(vmem_limit_bytes=VMEM_LIMIT),
        name="fock_rows",
    )(slots, owner_mask, every, all_points, params).reshape(rows_here, width)


def solution(mesh):
    return jax.shard_map(
        on_device,
        mesh=mesh,
        in_specs=(
            P("grid", "col"),
            P(None, "grid"),
            P("grid"),
            P(None, "col"),
            P("col"),
            P("grid", None, None),
            P("grid", None),
            P(),
            P("grid", "col"),
            P("grid", "col"),
        ),
        out_specs=P("grid", "col"),
        check_vma=False,
    )
```

```python
import functools
import math

import jax
import jax.numpy as jnp
from jax import lax
from jax.experimental import pallas as pl
from jax.experimental.pallas import tpu as pltpu
from jax.sharding import PartitionSpec as P

BLK = 128
CAPB = 2
MESH = pl.DeviceIdType.MESH
VMEM_LIMIT = 57 * 1024 * 1024

quad_nodes = 8


def boys_sum(argument):
    first = jnp.exp(argument * (-0.25 / (quad_nodes * quad_nodes)))
    ratio = jnp.exp(argument * (-2.0 / (quad_nodes * quad_nodes)))
    powers = [ratio]
    for _ in range(quad_nodes - 2):
        powers.append(powers[-1] * ratio)
    summed = 1.0 + powers[-1]
    for power in powers[-2::-1]:
        summed = 1.0 + power * summed
    return first * summed


def three_pieces(values):
    high = values.astype(jnp.bfloat16).astype(jnp.float32)
    rest = values - high
    middle = rest.astype(jnp.bfloat16).astype(jnp.float32)
    return jnp.concatenate([high, middle, rest - middle], axis=0).astype(jnp.bfloat16)


def picked(pieces, pick):
    out = jnp.dot(pieces, pick, preferred_element_type=jnp.float32)
    return out[0:8] + out[8:16] + out[16:24]


def one_hot(ids, count):
    rows = lax.broadcasted_iota(jnp.int32, (count, ids.shape[1]), 0)
    return jnp.where(rows == ids, 1.0, 0.0).astype(jnp.bfloat16)


def exchange_kernel(
    owners, cols, full,
    slot_ref, mask_ref, owner_mask_ref, density_ref, params_ref, win_c_ref, win_e_ref, points_ref, weights_ref,
    target_ref, source_ref,
    partial_ref,
    every, all_points, tile_send, tile_recv, msg_send, msg_recv, win_buf, spots, pair_scr, source_hot, target_hot, field, parts, parts_recv,
    tile_ss, tile_rs, msg_ss, msg_rs, win_ss, win_rs, part_ss, part_rs, every_ss, every_rs,
):
    me = lax.axis_index("grid")
    mc = lax.axis_index("col")
    batches, pairs = target_ref.shape
    pts = points_ref.shape[2]
    width = density_ref.shape[2]
    window = cols * width
    chunk = 256
    x, y, z = lax.rem(me, 2), lax.rem(me // 2, 2), me // 4
    deep = owners // 4
    half_batches = batches // 2
    half = half_batches * pts

    barrier = pltpu.get_barrier_semaphore()

    def greet_grid(j, carry):
        pl.semaphore_signal(
            barrier, inc=1, device_id={"grid": lax.rem(me + j, owners), "col": mc}, device_id_type=MESH
        )
        return carry

    def greet_col(j, carry):
        pl.semaphore_signal(
            barrier, inc=1, device_id={"grid": me, "col": lax.rem(mc + j, cols)}, device_id_type=MESH
        )
        return carry

    lax.fori_loop(1, owners, greet_grid, 0)
    lax.fori_loop(1, cols, greet_col, 0)

    def win_copy(j):
        return pltpu.make_async_remote_copy(
            src_ref=win_buf.at[mc], dst_ref=win_buf.at[mc], send_sem=win_ss.at[j], recv_sem=win_rs.at[j],
            device_id={"grid": me, "col": lax.rem(mc + j, cols)}, device_id_type=MESH,
        )

    def win_arrival(j):
        there = lax.rem(mc - j + cols, cols)
        return pltpu.make_async_remote_copy(
            src_ref=win_buf.at[there], dst_ref=win_buf.at[there], send_sem=win_ss.at[j], recv_sem=win_rs.at[j],
            device_id={"grid": me, "col": lax.rem(mc + j, cols)}, device_id_type=MESH,
        )

    def msg_copy(j):
        return pltpu.make_async_remote_copy(
            src_ref=msg_send.at[j], dst_ref=msg_recv.at[j], send_sem=msg_ss.at[j], recv_sem=msg_rs.at[j],
            device_id={"grid": lax.rem(me + j, owners), "col": mc}, device_id_type=MESH,
        )

    def tile_copy(j):
        return pltpu.make_async_remote_copy(
            src_ref=tile_send.at[j], dst_ref=tile_recv.at[j], send_sem=tile_ss.at[j], recv_sem=tile_rs.at[j],
            device_id={"grid": lax.rem(me + j, owners), "col": mc}, device_id_type=MESH,
        )

    def part_copy(j, h):
        there = lax.rem(mc + j, cols)
        rows = slice(h * half, (h + 1) * half)
        return pltpu.make_async_remote_copy(
            src_ref=parts.at[there, rows], dst_ref=parts_recv.at[j, rows], send_sem=part_ss.at[j, h],
            recv_sem=part_rs.at[j, h], device_id={"grid": me, "col": there}, device_id_type=MESH,
        )

    def spread_copy(user, h, peer, way):
        return pltpu.make_async_remote_copy(
            src_ref=every.at[user, h], dst_ref=every.at[user, h], send_sem=every_ss.at[way, h],
            recv_sem=every_rs.at[user, h], device_id={"grid": peer, "col": mc}, device_id_type=MESH,
        )

    def place(k, across_y, across_x):
        there_y = 1 - y if across_y else y
        there_x = 1 - x if across_x else x
        return (lax.rem(z + k, deep) * 2 + there_y) * 2 + there_x

    def send_x(user, h):
        spread_copy(user, h, place(0, False, True), 0).start()

    def send_y(user, h):
        spread_copy(user, h, place(0, True, False), 1).start()

    def arrived(user, h):
        spread_copy(user, h, place(0, False, True), 0).wait_recv()

    blank = jnp.zeros((4, BLK), jnp.float32)

    def add_fock(user, h):
        weighted = every[user, h]
        spot = all_points[user]
        for c in range(CAPB):
            block = slot_ref[user * CAPB + c]
            own = jnp.concatenate([params_ref[block], blank], axis=0).T
            held = [jnp.broadcast_to(own[:, a : a + 1], (BLK, BLK)) for a in range(4)]
            basis = []
            for b in range(h * half_batches, (h + 1) * half_batches):
                squared = None
                for a in range(3):
                    deltas = spot[3 * b + a : 3 * b + a + 1] - held[a]
                    squared = deltas * deltas if squared is None else squared + deltas * deltas
                value = jnp.exp(-held[3] * squared)
                if not full:
                    value = value * owner_mask_ref[(user * CAPB + c) * batches + b]
                basis.append(value.astype(jnp.bfloat16))
            partial_ref[user * CAPB + c] += jnp.dot(
                jnp.concatenate(basis, axis=1), weighted, preferred_element_type=jnp.float32
            )

    own_win = jnp.concatenate([win_c_ref[...], win_e_ref[...], jnp.zeros((4, width), jnp.float32)], axis=0)
    win_buf[mc] = own_win
    own_points = jnp.concatenate([points_ref[b] for b in range(batches)] + [weights_ref[...]], axis=0)

    def stage(j, tile_to, msg_to, index):
        peer = lax.rem(me + j, owners)
        rows = []
        for c in range(CAPB):
            block = slot_ref[peer * CAPB + c]
            tile_to[index, c * BLK : (c + 1) * BLK] = density_ref[block]
            rows.append(params_ref[block])
        msg_to[index] = jnp.concatenate(rows + [own_points], axis=0)

    stage(0, tile_recv, msg_recv, 0)
    pl.semaphore_wait(barrier, owners - 1 + cols - 1)

    for j in range(1, cols):
        win_copy(j).start()

    def send(j, carry):
        stage(j, tile_send, msg_send, j)
        msg_copy(j).start()
        tile_copy(j).start()
        return carry

    lax.fori_loop(1, owners, send, 0)

    columns = own_points.T
    for b in range(batches):
        for a in range(3):
            spots[a, b * pts : (b + 1) * pts] = jnp.broadcast_to(columns[:, 3 * b + a : 3 * b + a + 1], (pts, BLK))
        at = 3 * batches + b
        spots[3, b * pts : (b + 1) * pts] = jnp.broadcast_to(columns[:, at : at + 1], (pts, BLK))

    for j in range(1, cols):
        win_arrival(j).wait_recv()
    source_pieces = three_pieces(own_win)
    target_pieces = three_pieces(jnp.concatenate([win_buf[k] for k in range(cols)], axis=1))
    per_batch = pairs // chunk

    def pair_step(i, carry):
        b = i // per_batch
        lanes = pl.ds(pl.multiple_of(lax.rem(i, per_batch) * chunk, chunk), chunk)
        rows = pl.ds(pl.multiple_of(b * pts, pts), pts)
        target_pick = one_hot(target_ref[pl.ds(b, 1), lanes], window)
        source_pick = one_hot(source_ref[pl.ds(b, 1), lanes], width)
        target_hot[b, :, lanes] = target_pick
        source_hot[b, :, lanes] = source_pick
        tp = picked(target_pieces, target_pick)
        sp = picked(source_pieces, source_pick)
        te, se = tp[3:4], sp[3:4]
        joined = te + se
        separation = jnp.zeros_like(joined)
        centre = []
        for a in range(3):
            offset = tp[a : a + 1] - sp[a : a + 1]
            separation = separation + offset * offset
            centre.append((te * tp[a : a + 1] + se * sp[a : a + 1]) / joined)
        prefactor = (2.0 * math.pi / quad_nodes) / joined * jnp.exp(-te * se / joined * separation)
        out = []
        for h in range(chunk // BLK):
            part = slice(h * BLK, (h + 1) * BLK)
            spread = None
            for a in range(3):
                deltas = spots[a, rows] - centre[a][:, part]
                spread = deltas * deltas if spread is None else spread + deltas * deltas
            out.append(prefactor[:, part] * boys_sum(joined[:, part] * spread))
        pair_scr[rows, lanes] = jnp.concatenate(out, axis=1)
        return carry

    lax.fori_loop(0, batches * per_batch, pair_step, 0)

    field[...] = jnp.zeros_like(field)
    partial_ref[...] = jnp.zeros_like(partial_ref)

    def add_field(j):
        owner = lax.rem(me - j + owners, owners)
        params = msg_recv[j]
        all_points[owner] = params[8:24]
        tile = tile_recv[j]
        for b in range(batches):
            rows = slice(b * pts, (b + 1) * pts)
            halves = []
            for c in range(CAPB):
                squared = None
                for a in range(3):
                    deltas = spots[a, rows] - params[4 * c + a : 4 * c + a + 1]
                    squared = deltas * deltas if squared is None else squared + deltas * deltas
                value = jnp.exp(-params[4 * c + 3 : 4 * c + 4] * squared)
                if not full:
                    value = value * mask_ref[(b * owners + owner) * CAPB + c]
                halves.append(value.astype(jnp.bfloat16))
            basis = jnp.concatenate(halves, axis=1)
            field[rows] += jnp.dot(basis, tile, preferred_element_type=jnp.float32)

    add_field(0)

    def take(j, carry):
        msg_copy(j).wait_recv()
        tile_copy(j).wait_recv()
        add_field(j)
        return carry

    lax.fori_loop(1, owners, take, 0)

    def batch_step(b, carry):
        rows = pl.ds(pl.multiple_of(b * pts, pts), pts)
        values = field[rows].astype(jnp.bfloat16)
        total = jnp.zeros((pts, window), jnp.float32)
        for i in range(per_batch // 2):
            lanes = slice(i * 2 * chunk, (i + 1) * 2 * chunk)
            from_field = jnp.dot(values, source_hot[b, :, lanes], preferred_element_type=jnp.float32)
            product = (pair_scr[rows, lanes] * from_field).astype(jnp.bfloat16)
            total = total + lax.dot_general(
                product, target_hot[b, :, lanes], (((1,), (1,)), ((), ())), preferred_element_type=jnp.float32
            )
        for k in range(cols):
            parts[k, rows] = total[:, k * width : (k + 1) * width]
        return carry

    for h in range(2):
        lax.fori_loop(h * half_batches, (h + 1) * half_batches, batch_step, 0)
        for j in range(1, cols):
            part_copy(j, h).start()
    for h in range(2):
        rows = slice(h * half, (h + 1) * half)
        for j in range(1, cols):
            part_copy(j, h).wait_recv()
        potential = parts[mc, rows]
        for j in range(1, cols):
            potential = potential + parts_recv[j, rows]
        every[me, h] = (spots[3, rows] * potential).astype(jnp.bfloat16)
        send_x(me, h)
        send_y(me, h)
        for k in range(1, deep):
            spread_copy(me, h, place(k, False, False), 2).start()

    def forward_side(k):
        arrived(place(k, False, True), 0)
        send_y(place(k, False, True), 0)
        arrived(place(k, True, False), 1)
        send_x(place(k, True, False), 1)

    def add_side(k):
        add_fock(place(k, False, True), 0)
        add_fock(place(k, True, False), 1)

    add_fock(me, 0)
    add_fock(me, 1)

    def relay(k, carry):
        user = place(k, False, False)
        for h in range(2):
            arrived(user, h)
            send_x(user, h)
            send_y(user, h)
        forward_side(k - 1)
        add_fock(user, 0)
        add_fock(user, 1)
        add_side(k - 1)
        return carry

    lax.fori_loop(1, deep, relay, 0)
    forward_side(deep - 1)
    add_side(deep - 1)

    def last(k, carry):
        near = place(k, True, False), place(k, False, True)
        for h in range(2):
            arrived(near[h], h)
            add_fock(near[h], h)
        far = place(k, True, True)
        for h in range(2):
            arrived(far, h)
            add_fock(far, h)
        return carry

    lax.fori_loop(0, deep, last, 0)

    for j in range(1, cols):
        win_copy(j).wait_send()
        for h in range(2):
            part_copy(j, h).wait_send()

    for h in range(2):
        for way, sent in ((h, deep), (1 - h, 2 * deep), (2, deep - 1)):

            def drain_spread(k, carry, h=h, way=way):
                spread_copy(me, h, place(0, False, True), way).wait_send()
                return carry

            lax.fori_loop(0, sent, drain_spread, 0)

    def drain(j, carry):
        msg_copy(j).wait_send()
        tile_copy(j).wait_send()
        return carry

    lax.fori_loop(1, owners, drain, 0)


def fock_kernel(slot_ref, partial_ref, fock_ref):
    fock_ref[...] = jnp.zeros_like(fock_ref)

    def step(i, carry):
        fock_ref[slot_ref[i]] += partial_ref[i]
        return carry

    lax.fori_loop(0, partial_ref.shape[0], step, 0)


def on_device(
    density, row_centers, row_exps, win_centers, win_exps, points, weights, sig_blocks, pair_target, pair_source
):
    owners = lax.axis_size("grid")
    cols = lax.axis_size("col")
    me = lax.axis_index("grid")
    rows_here = row_exps.shape[0]
    held = rows_here // BLK
    width = density.shape[1]
    batches, _, pts = points.shape
    pairs = pair_target.shape[1]
    listed = sig_blocks.shape[1]
    full = listed == owners * CAPB
    count = batches * pts

    lists = sig_blocks.reshape(owners, batches * listed)
    local = lists - me * held
    mine = (local >= 0) & (local < held)
    low = jnp.min(jnp.where(mine, local, held), axis=1)
    high = jnp.max(jnp.where(mine, local, -1), axis=1)
    slots = jnp.clip(jnp.stack([low, high], axis=1), 0, held - 1).reshape(-1)
    if full:
        user_mask = owner_mask = jnp.zeros((1,), jnp.float32)
    else:
        my_lists = lax.dynamic_slice_in_dim(sig_blocks, me * batches, batches, 0)
        flat = my_lists.reshape(1, -1)
        of_owner = flat // held == jnp.arange(owners, dtype=jnp.int32)[:, None]
        least = jnp.min(jnp.where(of_owner, flat, owners * held), axis=1)
        most = jnp.max(jnp.where(of_owner, flat, -1), axis=1)
        most = jnp.where(most == least, -1, most)
        wanted = jnp.stack([least, most], axis=1)
        user_mask = jnp.any(my_lists[:, :, None, None] == wanted, axis=1).astype(jnp.float32).reshape(-1)
        ids = jnp.stack([low, jnp.where(high == low, -1, high)], axis=1)
        ids = jnp.where((ids >= 0) & (ids < held), ids + me * held, -1)
        by_batch = sig_blocks.reshape(owners, 1, batches, listed)
        owner_mask = jnp.any(by_batch == ids[:, :, None, None], axis=3).astype(jnp.float32).reshape(-1)

    smem = pl.BlockSpec(memory_space=pltpu.SMEM)
    vmem = pl.BlockSpec(memory_space=pltpu.VMEM)
    own_tiles = density.reshape(held, BLK, width)
    params = jnp.concatenate([row_centers, row_exps[None, :]], axis=0).reshape(4, held, BLK).transpose(1, 0, 2)
    partial = pl.pallas_call(
        functools.partial(exchange_kernel, owners, cols, full),
        out_shape=jax.ShapeDtypeStruct((owners * CAPB, BLK, width), jnp.float32),
        in_specs=[smem, smem, smem] + [vmem] * 8,
        out_specs=vmem,
        scratch_shapes=[
            pltpu.VMEM((owners, 2, count // 2, width), jnp.bfloat16),
            pltpu.VMEM((owners, 16, pts), jnp.float32),
            pltpu.VMEM((owners, CAPB * BLK, width), jnp.bfloat16),
            pltpu.VMEM((owners, CAPB * BLK, width), jnp.bfloat16),
            pltpu.VMEM((owners, 24, BLK), jnp.float32),
            pltpu.VMEM((owners, 24, BLK), jnp.float32),
            pltpu.VMEM((cols, 8, width), jnp.float32),
            pltpu.VMEM((4, count, BLK), jnp.float32),
            pltpu.VMEM((count, pairs), jnp.float32),
            pltpu.VMEM((batches, width, pairs), jnp.bfloat16),
            pltpu.VMEM((batches, cols * width, pairs), jnp.bfloat16),
            pltpu.VMEM((count, width), jnp.float32),
            pltpu.VMEM((cols, count, width), jnp.float32),
            pltpu.VMEM((cols, count, width), jnp.float32),
            pltpu.SemaphoreType.DMA((owners,)),
            pltpu.SemaphoreType.DMA((owners,)),
            pltpu.SemaphoreType.DMA((owners,)),
            pltpu.SemaphoreType.DMA((owners,)),
            pltpu.SemaphoreType.DMA((cols,)),
            pltpu.SemaphoreType.DMA((cols,)),
            pltpu.SemaphoreType.DMA((cols, 2)),
            pltpu.SemaphoreType.DMA((cols, 2)),
            pltpu.SemaphoreType.DMA((3, 2)),
            pltpu.SemaphoreType.DMA((owners, 2)),
        ],
        compiler_params=pltpu.CompilerParams(
            collective_id=0, has_side_effects=True, vmem_limit_bytes=VMEM_LIMIT
        ),
        name="exchange",
    )(
        slots, user_mask, owner_mask, own_tiles, params, win_centers, win_exps[None, :], points, weights,
        pair_target, pair_source,
    )
    return pl.pallas_call(
        fock_kernel,
        out_shape=jax.ShapeDtypeStruct((held, BLK, width), jnp.float32),
        in_specs=[smem, vmem],
        out_specs=vmem,
        compiler_params=pltpu.CompilerParams(vmem_limit_bytes=VMEM_LIMIT),
        name="fock_rows",
    )(slots, partial).reshape(rows_here, width)


def solution(mesh):
    return jax.shard_map(
        on_device,
        mesh=mesh,
        in_specs=(
            P("grid", "col"),
            P(None, "grid"),
            P("grid"),
            P(None, "col"),
            P("col"),
            P("grid", None, None),
            P("grid", None),
            P(),
            P("grid", "col"),
            P("grid", "col"),
        ),
        out_specs=P("grid", "col"),
        check_vma=False,
    )
```

```python
import functools
import math

import jax
import jax.numpy as jnp
from jax import lax
from jax.experimental import pallas as pl
from jax.experimental.pallas import tpu as pltpu
from jax.sharding import PartitionSpec as P

BLK = 128
CAPB = 2
MESH = pl.DeviceIdType.MESH
VMEM_LIMIT = 57 * 1024 * 1024

quad_nodes = 8


def boys_sum(argument):
    first = jnp.exp(argument * (-0.25 / (quad_nodes * quad_nodes)))
    ratio = jnp.exp(argument * (-2.0 / (quad_nodes * quad_nodes)))
    powers = [ratio]
    for _ in range(quad_nodes - 2):
        powers.append(powers[-1] * ratio)
    summed = 1.0 + powers[-1]
    for power in powers[-2::-1]:
        summed = 1.0 + power * summed
    return first * summed


def three_pieces(values):
    high = values.astype(jnp.bfloat16).astype(jnp.float32)
    rest = values - high
    middle = rest.astype(jnp.bfloat16).astype(jnp.float32)
    return jnp.concatenate([high, middle, rest - middle], axis=0).astype(jnp.bfloat16)


def picked(pieces, pick):
    out = jnp.dot(pieces, pick, preferred_element_type=jnp.float32)
    return out[0:8] + out[8:16] + out[16:24]


def one_hot(ids, count):
    rows = lax.broadcasted_iota(jnp.int32, (count, ids.shape[1]), 0)
    return jnp.where(rows == ids, 1.0, 0.0).astype(jnp.bfloat16)


def exchange_kernel(
    owners, cols, full,
    slot_ref, mask_ref, owner_mask_ref, density_ref, row_c_ref, row_e_ref, win_c_ref, win_e_ref, points_ref, weights_ref,
    target_ref, source_ref,
    partial_ref,
    params_scr, every, all_points, tile_send, tile_recv, msg_send, msg_recv, win_buf, spots, pair_scr, source_hot, target_hot, field, parts, parts_recv,
    tile_ss, tile_rs, msg_ss, msg_rs, win_ss, win_rs, part_ss, part_rs, every_ss, every_rs,
):
    me = lax.axis_index("grid")
    mc = lax.axis_index("col")
    batches, pairs = target_ref.shape
    pts = points_ref.shape[2]
    width = density_ref.shape[2]
    window = cols * width
    chunk = 256
    x, y, z = lax.rem(me, 2), lax.rem(me // 2, 2), me // 4
    deep = owners // 4
    half_batches = batches // 2
    half = half_batches * pts

    for i in range(params_scr.shape[0]):
        lanes = slice(i * BLK, (i + 1) * BLK)
        params_scr[i] = jnp.concatenate([row_c_ref[:, lanes], row_e_ref[:, lanes]], axis=0)

    barrier = pltpu.get_barrier_semaphore()

    def greet_grid(j, carry):
        pl.semaphore_signal(
            barrier, inc=1, device_id={"grid": lax.rem(me + j, owners), "col": mc}, device_id_type=MESH
        )
        return carry

    def greet_col(j, carry):
        pl.semaphore_signal(
            barrier, inc=1, device_id={"grid": me, "col": lax.rem(mc + j, cols)}, device_id_type=MESH
        )
        return carry

    lax.fori_loop(1, owners, greet_grid, 0)
    lax.fori_loop(1, cols, greet_col, 0)

    def win_copy(j):
        return pltpu.make_async_remote_copy(
            src_ref=win_buf.at[mc], dst_ref=win_buf.at[mc], send_sem=win_ss.at[j], recv_sem=win_rs.at[j],
            device_id={"grid": me, "col": lax.rem(mc + j, cols)}, device_id_type=MESH,
        )

    def win_arrival(j):
        there = lax.rem(mc - j + cols, cols)
        return pltpu.make_async_remote_copy(
            src_ref=win_buf.at[there], dst_ref=win_buf.at[there], send_sem=win_ss.at[j], recv_sem=win_rs.at[j],
            device_id={"grid": me, "col": lax.rem(mc + j, cols)}, device_id_type=MESH,
        )

    def msg_copy(j):
        return pltpu.make_async_remote_copy(
            src_ref=msg_send.at[j], dst_ref=msg_recv.at[j], send_sem=msg_ss.at[j], recv_sem=msg_rs.at[j],
            device_id={"grid": lax.rem(me + j, owners), "col": mc}, device_id_type=MESH,
        )

    def tile_copy(j):
        return pltpu.make_async_remote_copy(
            src_ref=tile_send.at[j], dst_ref=tile_recv.at[j], send_sem=tile_ss.at[j], recv_sem=tile_rs.at[j],
            device_id={"grid": lax.rem(me + j, owners), "col": mc}, device_id_type=MESH,
        )

    def part_copy(j, h):
        there = lax.rem(mc + j, cols)
        rows = slice(h * half, (h + 1) * half)
        return pltpu.make_async_remote_copy(
            src_ref=parts.at[there, rows], dst_ref=parts_recv.at[j, rows], send_sem=part_ss.at[j, h],
            recv_sem=part_rs.at[j, h], device_id={"grid": me, "col": there}, device_id_type=MESH,
        )

    def spread_copy(user, h, peer, way):
        return pltpu.make_async_remote_copy(
            src_ref=every.at[user, h], dst_ref=every.at[user, h], send_sem=every_ss.at[way, h],
            recv_sem=every_rs.at[user, h], device_id={"grid": peer, "col": mc}, device_id_type=MESH,
        )

    def place(k, across_y, across_x):
        there_y = 1 - y if across_y else y
        there_x = 1 - x if across_x else x
        return (lax.rem(z + k, deep) * 2 + there_y) * 2 + there_x

    def send_x(user, h):
        spread_copy(user, h, place(0, False, True), 0).start()

    def send_y(user, h):
        spread_copy(user, h, place(0, True, False), 1).start()

    def arrived(user, h):
        spread_copy(user, h, place(0, False, True), 0).wait_recv()

    blank = jnp.zeros((4, BLK), jnp.float32)

    def add_fock(user, h):
        weighted = every[user, h]
        spot = all_points[user]
        for c in range(CAPB):
            block = slot_ref[user * CAPB + c]
            own = jnp.concatenate([params_scr[block], blank], axis=0).T
            held = [jnp.broadcast_to(own[:, a : a + 1], (BLK, BLK)) for a in range(4)]
            basis = []
            for b in range(h * half_batches, (h + 1) * half_batches):
                squared = None
                for a in range(3):
                    deltas = spot[3 * b + a : 3 * b + a + 1] - held[a]
                    squared = deltas * deltas if squared is None else squared + deltas * deltas
                value = jnp.exp(-held[3] * squared)
                if not full:
                    value = value * owner_mask_ref[(user * CAPB + c) * batches + b]
                basis.append(value.astype(jnp.bfloat16))
            partial_ref[user * CAPB + c] += jnp.dot(
                jnp.concatenate(basis, axis=1), weighted, preferred_element_type=jnp.float32
            )

    own_win = jnp.concatenate([win_c_ref[...], win_e_ref[...], jnp.zeros((4, width), jnp.float32)], axis=0)
    win_buf[mc] = own_win
    own_points = jnp.concatenate([points_ref[b] for b in range(batches)] + [weights_ref[...]], axis=0)

    def stage(j, tile_to, msg_to, index):
        peer = lax.rem(me + j, owners)
        rows = []
        for c in range(CAPB):
            block = slot_ref[peer * CAPB + c]
            tile_to[index, c * BLK : (c + 1) * BLK] = density_ref[block]
            rows.append(params_scr[block])
        msg_to[index] = jnp.concatenate(rows + [own_points], axis=0)

    stage(0, tile_recv, msg_recv, 0)
    pl.semaphore_wait(barrier, owners - 1 + cols - 1)

    for j in range(1, cols):
        win_copy(j).start()

    def send(j, carry):
        stage(j, tile_send, msg_send, j)
        msg_copy(j).start()
        tile_copy(j).start()
        return carry

    lax.fori_loop(1, owners, send, 0)

    columns = own_points.T
    for b in range(batches):
        for a in range(3):
            spots[a, b * pts : (b + 1) * pts] = jnp.broadcast_to(columns[:, 3 * b + a : 3 * b + a + 1], (pts, BLK))
        at = 3 * batches + b
        spots[3, b * pts : (b + 1) * pts] = jnp.broadcast_to(columns[:, at : at + 1], (pts, BLK))

    for j in range(1, cols):
        win_arrival(j).wait_recv()
    source_pieces = three_pieces(own_win)
    target_pieces = three_pieces(jnp.concatenate([win_buf[k] for k in range(cols)], axis=1))
    per_batch = pairs // chunk

    def pair_step(i, carry):
        b = i // per_batch
        lanes = pl.ds(pl.multiple_of(lax.rem(i, per_batch) * chunk, chunk), chunk)
        rows = pl.ds(pl.multiple_of(b * pts, pts), pts)
        target_pick = one_hot(target_ref[pl.ds(b, 1), lanes], window)
        source_pick = one_hot(source_ref[pl.ds(b, 1), lanes], width)
        target_hot[b, :, lanes] = target_pick
        source_hot[b, :, lanes] = source_pick
        tp = picked(target_pieces, target_pick)
        sp = picked(source_pieces, source_pick)
        te, se = tp[3:4], sp[3:4]
        joined = te + se
        separation = jnp.zeros_like(joined)
        centre = []
        for a in range(3):
            offset = tp[a : a + 1] - sp[a : a + 1]
            separation = separation + offset * offset
            centre.append((te * tp[a : a + 1] + se * sp[a : a + 1]) / joined)
        prefactor = (2.0 * math.pi / quad_nodes) / joined * jnp.exp(-te * se / joined * separation)
        out = []
        for h in range(chunk // BLK):
            part = slice(h * BLK, (h + 1) * BLK)
            spread = None
            for a in range(3):
                deltas = spots[a, rows] - centre[a][:, part]
                spread = deltas * deltas if spread is None else spread + deltas * deltas
            out.append(prefactor[:, part] * boys_sum(joined[:, part] * spread))
        pair_scr[rows, lanes] = jnp.concatenate(out, axis=1)
        return carry

    lax.fori_loop(0, batches * per_batch, pair_step, 0)

    field[...] = jnp.zeros_like(field)
    partial_ref[...] = jnp.zeros_like(partial_ref)

    def add_field(j):
        owner = lax.rem(me - j + owners, owners)
        params = msg_recv[j]
        all_points[owner] = params[8:24]
        tile = tile_recv[j]
        for b in range(batches):
            rows = slice(b * pts, (b + 1) * pts)
            halves = []
            for c in range(CAPB):
                squared = None
                for a in range(3):
                    deltas = spots[a, rows] - params[4 * c + a : 4 * c + a + 1]
                    squared = deltas * deltas if squared is None else squared + deltas * deltas
                value = jnp.exp(-params[4 * c + 3 : 4 * c + 4] * squared)
                if not full:
                    value = value * mask_ref[(b * owners + owner) * CAPB + c]
                halves.append(value.astype(jnp.bfloat16))
            basis = jnp.concatenate(halves, axis=1)
            field[rows] += jnp.dot(basis, tile, preferred_element_type=jnp.float32)

    add_field(0)

    def take(j, carry):
        msg_copy(j).wait_recv()
        tile_copy(j).wait_recv()
        add_field(j)
        return carry

    lax.fori_loop(1, owners, take, 0)

    def batch_step(b, carry):
        rows = pl.ds(pl.multiple_of(b * pts, pts), pts)
        values = field[rows].astype(jnp.bfloat16)
        total = jnp.zeros((pts, window), jnp.float32)
        for i in range(per_batch // 2):
            lanes = slice(i * 2 * chunk, (i + 1) * 2 * chunk)
            from_field = jnp.dot(values, source_hot[b, :, lanes], preferred_element_type=jnp.float32)
            product = (pair_scr[rows, lanes] * from_field).astype(jnp.bfloat16)
            total = total + lax.dot_general(
                product, target_hot[b, :, lanes], (((1,), (1,)), ((), ())), preferred_element_type=jnp.float32
            )
        for k in range(cols):
            parts[k, rows] = total[:, k * width : (k + 1) * width]
        return carry

    for h in range(2):
        lax.fori_loop(h * half_batches, (h + 1) * half_batches, batch_step, 0)
        for j in range(1, cols):
            part_copy(j, h).start()
    for h in range(2):
        rows = slice(h * half, (h + 1) * half)
        for j in range(1, cols):
            part_copy(j, h).wait_recv()
        potential = parts[mc, rows]
        for j in range(1, cols):
            potential = potential + parts_recv[j, rows]
        every[me, h] = (spots[3, rows] * potential).astype(jnp.bfloat16)
        send_x(me, h)
        send_y(me, h)
        for k in range(1, deep):
            spread_copy(me, h, place(k, False, False), 2).start()

    def forward_side(k):
        arrived(place(k, False, True), 0)
        send_y(place(k, False, True), 0)
        arrived(place(k, True, False), 1)
        send_x(place(k, True, False), 1)

    def add_side(k):
        add_fock(place(k, False, True), 0)
        add_fock(place(k, True, False), 1)

    add_fock(me, 0)
    add_fock(me, 1)

    def relay(k, carry):
        user = place(k, False, False)
        for h in range(2):
            arrived(user, h)
            send_x(user, h)
            send_y(user, h)
        add_fock(user, 0)
        forward_side(k - 1)
        add_fock(user, 1)
        add_side(k - 1)
        return carry

    lax.fori_loop(1, deep, relay, 0)
    forward_side(deep - 1)
    add_side(deep - 1)

    def last(k, carry):
        near = place(k, True, False), place(k, False, True)
        for h in range(2):
            arrived(near[h], h)
            add_fock(near[h], h)
        far = place(k, True, True)
        for h in range(2):
            arrived(far, h)
            add_fock(far, h)
        return carry

    lax.fori_loop(0, deep, last, 0)

    for j in range(1, cols):
        win_copy(j).wait_send()
        for h in range(2):
            part_copy(j, h).wait_send()

    for h in range(2):
        for way, sent in ((h, deep), (1 - h, 2 * deep), (2, deep - 1)):

            def drain_spread(k, carry, h=h, way=way):
                spread_copy(me, h, place(0, False, True), way).wait_send()
                return carry

            lax.fori_loop(0, sent, drain_spread, 0)

    def drain(j, carry):
        msg_copy(j).wait_send()
        tile_copy(j).wait_send()
        return carry

    lax.fori_loop(1, owners, drain, 0)


def fock_kernel(slot_ref, partial_ref, fock_ref):
    fock_ref[...] = jnp.zeros_like(fock_ref)

    def step(i, carry):
        fock_ref[slot_ref[i]] += partial_ref[i]
        return carry

    lax.fori_loop(0, partial_ref.shape[0], step, 0)


def on_device(
    density, row_centers, row_exps, win_centers, win_exps, points, weights, sig_blocks, pair_target, pair_source
):
    owners = lax.axis_size("grid")
    cols = lax.axis_size("col")
    me = lax.axis_index("grid")
    rows_here = row_exps.shape[0]
    held = rows_here // BLK
    width = density.shape[1]
    batches, _, pts = points.shape
    pairs = pair_target.shape[1]
    listed = sig_blocks.shape[1]
    full = listed == owners * CAPB
    count = batches * pts

    lists = sig_blocks.reshape(owners, batches * listed)
    local = lists - me * held
    mine = (local >= 0) & (local < held)
    low = jnp.min(jnp.where(mine, local, held), axis=1)
    high = jnp.max(jnp.where(mine, local, -1), axis=1)
    slots = jnp.clip(jnp.stack([low, high], axis=1), 0, held - 1).reshape(-1)
    if full:
        user_mask = owner_mask = jnp.zeros((1,), jnp.float32)
    else:
        my_lists = lax.dynamic_slice_in_dim(sig_blocks, me * batches, batches, 0)
        flat = my_lists.reshape(1, -1)
        of_owner = flat // held == jnp.arange(owners, dtype=jnp.int32)[:, None]
        least = jnp.min(jnp.where(of_owner, flat, owners * held), axis=1)
        most = jnp.max(jnp.where(of_owner, flat, -1), axis=1)
        most = jnp.where(most == least, -1, most)
        wanted = jnp.stack([least, most], axis=1)
        user_mask = jnp.any(my_lists[:, :, None, None] == wanted, axis=1).astype(jnp.float32).reshape(-1)
        ids = jnp.stack([low, jnp.where(high == low, -1, high)], axis=1)
        ids = jnp.where((ids >= 0) & (ids < held), ids + me * held, -1)
        by_batch = sig_blocks.reshape(owners, 1, batches, listed)
        owner_mask = jnp.any(by_batch == ids[:, :, None, None], axis=3).astype(jnp.float32).reshape(-1)

    smem = pl.BlockSpec(memory_space=pltpu.SMEM)
    vmem = pl.BlockSpec(memory_space=pltpu.VMEM)
    own_tiles = density.reshape(held, BLK, width)
    partial = pl.pallas_call(
        functools.partial(exchange_kernel, owners, cols, full),
        out_shape=jax.ShapeDtypeStruct((owners * CAPB, BLK, width), jnp.float32),
        in_specs=[smem, smem, smem] + [vmem] * 9,
        out_specs=vmem,
        scratch_shapes=[
            pltpu.VMEM((held, 4, BLK), jnp.float32),
            pltpu.VMEM((owners, 2, count // 2, width), jnp.bfloat16),
            pltpu.VMEM((owners, 16, pts), jnp.float32),
            pltpu.VMEM((owners, CAPB * BLK, width), jnp.bfloat16),
            pltpu.VMEM((owners, CAPB * BLK, width), jnp.bfloat16),
            pltpu.VMEM((owners, 24, BLK), jnp.float32),
            pltpu.VMEM((owners, 24, BLK), jnp.float32),
            pltpu.VMEM((cols, 8, width), jnp.float32),
            pltpu.VMEM((4, count, BLK), jnp.float32),
            pltpu.VMEM((count, pairs), jnp.float32),
            pltpu.VMEM((batches, width, pairs), jnp.bfloat16),
            pltpu.VMEM((batches, cols * width, pairs), jnp.bfloat16),
            pltpu.VMEM((count, width), jnp.float32),
            pltpu.VMEM((cols, count, width), jnp.float32),
            pltpu.VMEM((cols, count, width), jnp.float32),
            pltpu.SemaphoreType.DMA((owners,)),
            pltpu.SemaphoreType.DMA((owners,)),
            pltpu.SemaphoreType.DMA((owners,)),
            pltpu.SemaphoreType.DMA((owners,)),
            pltpu.SemaphoreType.DMA((cols,)),
            pltpu.SemaphoreType.DMA((cols,)),
            pltpu.SemaphoreType.DMA((cols, 2)),
            pltpu.SemaphoreType.DMA((cols, 2)),
            pltpu.SemaphoreType.DMA((3, 2)),
            pltpu.SemaphoreType.DMA((owners, 2)),
        ],
        compiler_params=pltpu.CompilerParams(
            collective_id=0, has_side_effects=True, vmem_limit_bytes=VMEM_LIMIT
        ),
        name="exchange",
    )(
        slots, user_mask, owner_mask, own_tiles, row_centers, row_exps[None, :], win_centers, win_exps[None, :], points, weights,
        pair_target, pair_source,
    )
    return pl.pallas_call(
        fock_kernel,
        out_shape=jax.ShapeDtypeStruct((held, BLK, width), jnp.float32),
        in_specs=[smem, vmem],
        out_specs=vmem,
        compiler_params=pltpu.CompilerParams(vmem_limit_bytes=VMEM_LIMIT),
        name="fock_rows",
    )(slots, partial).reshape(rows_here, width)


def solution(mesh):
    return jax.shard_map(
        on_device,
        mesh=mesh,
        in_specs=(
            P("grid", "col"),
            P(None, "grid"),
            P("grid"),
            P(None, "col"),
            P("col"),
            P("grid", None, None),
            P("grid", None),
            P(),
            P("grid", "col"),
            P("grid", "col"),
        ),
        out_specs=P("grid", "col"),
        check_vma=False,
    )
```
